512 devices in a mesh: req: 32 (over z, x), tp: 16 (over y, core).
Axes of the slice: x: 4, y: 8, z: 8, core: 2. Of those that a mesh axis runs over, the one named last changes fastest.
Arguments:
- tokens: bfloat16 [8192, 8192], P('req', 'tp'), may hold values from -6 to 6
- w_inner: bfloat16 [8192, 8192], P('req', 'tp'), may hold values from -0.0625 to 0.0625
- w_bc: bfloat16 [8192, 32], replicated, may hold values from -0.0625 to 0.0625
- w_dt_down: bfloat16 [8192, 512], P(None, 'tp'), may hold values from -0.0625 to 0.0625
- w_dt_up: bfloat16 [512, 8192], P(None, 'tp'), may hold values from -0.25 to 0.25
- step_bias: float32 [8192], P('tp'), may hold values from -4 to 0
- decay_rate: float32 [16, 8192], P(None, 'tp'), may hold values from 0.01 to 4
- skip_gain: float32 [8192], P('tp'), may hold values from 0.5 to 1.5
- norm_gain: float32 [8192], P('tp'), may hold values from 0.5 to 1.5
- cache: float32 [32, 16, 16, 8192], P('req', None, None, 'tp'), may hold values from -6 to 6
- hits: int32 [32, 2], replicated, may hold values from 0 to 31, as said below
Outputs:
- normed: bfloat16 [8192, 8192], P('req', 'tp')
- last_state: float32 [32, 16, 8192], P('req', None, 'tp')
The draws below stay inside these ranges and needn't reach their ends.
Inputs may be any that keep to these rules, and one draw needn't show every extreme that they name: hits[r, 0] is an index of req in 0 to 32 - 1 and hits[r, 1] a prefix length of 1 to 16 blocks; some request has 16 blocks, some prefix is held by index 0 and some by the last index of req.
All inputs are finite; a program needn't handle non-finite values.
Results may differ from the reference program's by a relative error of at most 0.0055.
Values may be sent and summed in bfloat16 or wider, within the bound.
No kernel may reach another device: no remote copies, remote signals or barrier semaphores. Data moves between devices by JAX's collectives and lax.ppermute only.
A program may use at most 64 MiB of HBM per device.

```python
import math
import jax
import jax.numpy as jnp
from jax import lax

D = 8192
E = 8192
STATE = 16
DT_RANK = 512
MAXC = 16
TOK = 256
TOKENS = 8192
N_REQ = 32


def draw_hits(key, part):
    key = jax.random.fold_in(key, 7)
    first, second, third = jax.random.split(key, 3)
    picks = jax.random.randint(first, (N_REQ,), 0, N_REQ)
    order = jax.random.permutation(second, N_REQ)
    owner = order[picks * picks // N_REQ]
    owner = owner.at[1].set(N_REQ - 1)
    owner = owner.at[2].set(0)
    length = jax.random.randint(third, (N_REQ,), 1, MAXC + 1)
    length = length.at[0].set(MAXC)
    return jnp.stack([owner, length], axis=1).astype(jnp.int32)


def level_of(own_key, shape, shards, smallest, largest):
    factor_of, own = 1.0, jax.random.fold_in(own_key, 6)
    for axis_at, parts in shards:
        heights = jnp.exp(jax.random.uniform(jax.random.fold_in(own, axis_at), (parts,), jnp.float32, smallest / len(shards), largest / len(shards)))
        factor_of = factor_of * jnp.repeat(heights, shape[axis_at] // parts).reshape([-1 if axis == axis_at else 1 for axis in range(len(shape))])
    return factor_of


def normal_values(rng, shape, width, reach, pieces=(), held_as=jnp.bfloat16):
    values = width * jax.random.normal(rng, shape, jnp.float32)
    if pieces:
        values = values * level_of(rng, shape, pieces, -0.22, 0.18)
    return jnp.clip(values, -reach, reach).astype(held_as)


def setup_inputs(seed: int = 0) -> dict:
    seeds = jax.random.split(jax.random.key(seed), 12)
    return {
        "tokens": normal_values(seeds[0], (TOKENS, D), 1.0, 6.0, ((0, 32), (1, 16))),
        "w_inner": normal_values(seeds[1], (D, E), D ** -0.5, 0.0625, ((0, 32), (1, 16))),
        "w_bc": normal_values(seeds[2], (D, 2 * STATE), D ** -0.5, 0.0625),
        "w_dt_down": normal_values(seeds[3], (D, DT_RANK), D ** -0.5, 0.0625, ((1, 16),)),
        "w_dt_up": normal_values(seeds[4], (DT_RANK, E), DT_RANK ** -0.5, 0.25, ((1, 16),)),
        "step_bias": jnp.clip(-4.0 + 4.0 * jax.random.uniform(seeds[5], (E,), jnp.float32) ** level_of(seeds[5], (E,), ((0, 16),), -0.2, 0.2), -4.0, 0.0),
        "decay_rate": jnp.clip(jnp.exp(math.log(4.0) - 5.9914646 * jax.random.uniform(seeds[6], (STATE, E), jnp.float32) ** level_of(seeds[6], (STATE, E), ((1, 16),), -0.2, 0.2)), 0.01, 4.0),
        "skip_gain": jnp.clip(0.5 + 1.0 * jax.random.uniform(seeds[7], (E,), jnp.float32) ** level_of(seeds[7], (E,), ((0, 16),), -0.2, 0.2), 0.5, 1.5),
        "norm_gain": jnp.clip(1.0 + 0.1 * jax.random.normal(seeds[8], (E,), jnp.float32), 0.5, 1.5),
        "cache": normal_values(seeds[9], (N_REQ, MAXC, STATE, E), 1.0, 6.0, ((0, 32), (3, 16)), jnp.float32),
        "hits": draw_hits(jax.random.fold_in(seeds[11], 71), 0),
    }


def reference(tokens, w_inner, w_bc, w_dt_down, w_dt_up, step_bias, decay_rate, skip_gain, norm_gain, cache, hits):
    inner = jax.nn.silu(jnp.dot(tokens, w_inner, preferred_element_type=jnp.float32)).astype(jnp.bfloat16)
    maps = jnp.dot(tokens, w_bc, preferred_element_type=jnp.float32)
    in_map = maps[:, :STATE]
    out_map = maps[:, STATE:]
    low = jnp.dot(tokens, w_dt_down, preferred_element_type=jnp.float32).astype(jnp.bfloat16)
    step = jax.nn.softplus(jnp.dot(low, w_dt_up, preferred_element_type=jnp.float32) + step_bias[None, :])
    owner = hits[:, 0].astype(jnp.int32)
    length = hits[:, 1].astype(jnp.int32)
    state_init = cache[owner, length - 1]
    values = inner.astype(jnp.float32).reshape(N_REQ, TOK, E).transpose(1, 0, 2)
    ins = in_map.reshape(N_REQ, TOK, STATE).transpose(1, 0, 2)
    outs = out_map.reshape(N_REQ, TOK, STATE).transpose(1, 0, 2)
    steps = step.reshape(N_REQ, TOK, E).transpose(1, 0, 2)

    def advance(state, item):
        value, bvec, cvec, delta = item
        decay = jnp.exp(-decay_rate[None, :, :] * delta[:, None, :])
        state = decay * state + bvec[:, :, None] * (delta * value)[:, None, :]
        result = lax.optimization_barrier(jnp.sum(cvec[:, :, None] * state, axis=1)) + skip_gain[None, :] * value
        return (state, result)
    final, results = lax.scan(advance, state_init, (values, ins, outs, steps))
    out = results.transpose(1, 0, 2).reshape(TOKENS, E)
    scale = lax.rsqrt(lax.optimization_barrier(jnp.mean(out * out, axis=1)) + 1e-05)
    normed = (out * scale[:, None] * norm_gain[None, :]).astype(jnp.bfloat16)
    return (normed, final)
```

```python
import jax
import jax.numpy as jnp
from jax import lax
from jax.experimental import pallas as pl
from jax.experimental.pallas import tpu as pltpu
from jax.sharding import PartitionSpec as P

LOG2E = 1.4426950408889634
GROUP = 8


def scan_kernel(values, steps, ins, outs, decay, skip, start, out, state, squares):
    rows, width = out.shape
    rate = decay[...] * -LOG2E
    gain = skip[...]
    line = lax.broadcasted_iota(jnp.int32, (GROUP, width), 0)

    def merge(low, high, bit):
        upper = (line & bit) != 0
        kept = jnp.where(upper, high, low)
        moved = jnp.where(upper, low, high)
        return kept + pltpu.roll(moved, GROUP - bit, 0)

    def advance(index, held):
        first = pl.multiple_of(index * GROUP, GROUP)
        value = values[pl.ds(first, GROUP), :].astype(jnp.float32)
        step = steps[pl.ds(first, GROUP), :]
        fed = step * value
        terms = []
        for at in range(GROUP):
            factor = jnp.exp2(rate * step[at : at + 1, :])
            into = jnp.tile(ins[first + at], (1, width // 128))
            held = factor * held + into * fed[at : at + 1, :]
            onto = jnp.tile(outs[first + at], (1, width // 128)) * held
            terms.append(onto[:GROUP] + onto[GROUP:])
        for bit in (1, 2, 4):
            terms = [merge(low, high, bit) for low, high in zip(terms[::2], terms[1::2])]
        out[pl.ds(first, GROUP), :] = terms[0] + gain * value
        return held

    state[...] = lax.fori_loop(0, rows // GROUP, advance, start[...].astype(jnp.float32))
    whole = out[...]
    ones = jnp.ones((squares.shape[0], width), jnp.float32)
    squares[...] = lax.dot_general(
        ones,
        whole * whole,
        (((1,), (1,)), ((), ())),
        precision=lax.Precision.HIGHEST,
        preferred_element_type=jnp.float32,
    )


def run_scan(values, steps, ins, outs, decay, skip, start, copies):
    rows, width = values.shape
    cells = rows * width * decay.shape[0]
    return pl.pallas_call(
        scan_kernel,
        out_shape=(
            jax.ShapeDtypeStruct((rows, width), jnp.float32),
            jax.ShapeDtypeStruct(decay.shape, jnp.float32),
            jax.ShapeDtypeStruct((copies, rows), jnp.float32),
        ),
        compiler_params=pltpu.CompilerParams(vmem_limit_bytes=32 * 1024 * 1024),
        cost_estimate=pl.CostEstimate(flops=8 * cells, bytes_accessed=8 << 20, transcendentals=cells),
    )(values, steps, ins, outs, decay, skip, start)


def ring(block, axis, forward, backward, turns):
    half = block.shape[0] // 2
    after, before = [block], []
    left = right = block
    for _ in range(turns // 2 - 1):
        left = lax.ppermute(left, axis, forward)
        right = lax.ppermute(right, axis, backward)
        after.append(left)
        before.append(right)
    far = jnp.concatenate(
        [lax.ppermute(left[:half], axis, forward), lax.ppermute(right[half:], axis, backward)], axis=0
    )
    return jnp.stack(after + [far] + before[::-1], axis=0)


def per_device(
    tokens,
    w_inner,
    w_bc,
    w_dt_down,
    w_dt_up,
    step_bias,
    decay_rate,
    skip_gain,
    norm_gain,
    cache,
    hits,
):
    rows, share = tokens.shape
    width = w_inner.shape[1]
    parts = lax.axis_size("tp")
    chips = parts // 2
    place = lax.axis_index("tp")
    full_weight = lax.all_gather(w_inner, "req", axis=0, tiled=True)

    up = [(2 * y + c, 2 * ((y + 1) % chips) + c) for y in range(chips) for c in range(2)]
    down = [(b, a) for a, b in up]
    swap = [(i, i ^ 1) for i in range(parts)]
    mine = ring(tokens, "tp", up, down, chips)
    other = lax.ppermute(mine, "tp", swap)
    core = place % 2
    pair = jnp.where(
        core == 0, jnp.stack([mine, other], axis=1), jnp.stack([other, mine], axis=1)
    )
    order = (place // 2 - jnp.arange(chips)) % chips
    whole = jnp.transpose(jnp.take(pair, order, axis=0), (2, 0, 1, 3)).reshape(rows, parts * share)

    here = lax.axis_index("req")
    states = jnp.take(cache[0].astype(jnp.bfloat16), hits[:, 1] - 1, axis=0)
    arrived = lax.all_to_all(states, "req", split_axis=0, concat_axis=0, tiled=True)
    start = lax.dynamic_index_in_dim(arrived, hits[here, 0], axis=0, keepdims=False)

    state_size = decay_rate.shape[0]
    maps = jnp.dot(whole, w_bc, preferred_element_type=jnp.float32)
    spread = jnp.broadcast_to(maps[:, :, None], (rows, 2 * state_size, 128))
    low_part = jnp.dot(whole, w_dt_down, preferred_element_type=jnp.float32).astype(jnp.bfloat16)
    low = lax.all_gather(low_part, "tp", axis=1, tiled=True)
    step = jax.nn.softplus(
        jnp.dot(low, w_dt_up, preferred_element_type=jnp.float32) + step_bias[None, :]
    )

    projected = jnp.dot(whole, full_weight, preferred_element_type=jnp.float32)
    inner = jax.nn.silu(projected).astype(jnp.bfloat16)
    out, state, squares = run_scan(
        inner,
        step,
        spread[:, :state_size],
        spread[:, state_size:],
        decay_rate,
        skip_gain[None, :],
        start,
        parts,
    )
    sums = jnp.sum(lax.all_to_all(squares, "tp", split_axis=0, concat_axis=0, tiled=True), axis=0)
    scale = lax.rsqrt(sums / (width * parts) + 1e-05)
    normed = (out * scale[:, None] * norm_gain[None, :]).astype(jnp.bfloat16)
    return (normed, state.reshape(1, state_size, width))


def solution(mesh):
    placed = (
        P("req", "tp"),
        P("req", "tp"),
        P(),
        P(None, "tp"),
        P(None, "tp"),
        P("tp"),
        P(None, "tp"),
        P("tp"),
        P("tp"),
        P("req", None, None, "tp"),
        P(),
    )
    return jax.shard_map(
        per_device,
        mesh=mesh,
        in_specs=placed,
        out_specs=(P("req", "tp"), P("req", None, "tp")),
        check_vma=False,
    )
```

```python
import jax
import jax.numpy as jnp
from jax import lax
from jax.experimental import pallas as pl
from jax.experimental.pallas import tpu as pltpu
from jax.sharding import PartitionSpec as P

LOG2E = 1.4426950408889634
GROUP = 8


def scan_kernel(source, half, rest, steps, maps, decay, skip, starts, out, state, squares, values, begin, landed):
    rows, width = out.shape
    copy = pltpu.make_async_copy(starts.at[source[0]], begin, landed)
    copy.start()
    projected = half[...] + rest[...].astype(jnp.float32)
    inner = projected / (1.0 + jnp.exp(-projected))
    values[...] = inner.astype(jnp.bfloat16).astype(jnp.float32)
    rate = decay[...] * -LOG2E
    size = decay.shape[0]
    gain = skip[...]
    line = lax.broadcasted_iota(jnp.int32, (GROUP, width), 0)

    def merge(low, high, bit):
        upper = (line & bit) != 0
        kept = jnp.where(upper, high, low)
        moved = jnp.where(upper, low, high)
        return kept + pltpu.roll(moved, GROUP - bit, 0)

    def advance(index, held):
        first = pl.multiple_of(index * GROUP, GROUP)
        value = values[pl.ds(first, GROUP), :]
        step = steps[pl.ds(first, GROUP), :]
        fed = step * value
        terms = []
        for at in range(GROUP):
            factor = jnp.exp2(rate * step[at : at + 1, :])
            into = jnp.tile(maps[first + at, :size], (1, width // 128))
            held = factor * held + into * fed[at : at + 1, :]
            onto = jnp.tile(maps[first + at, size:], (1, width // 128)) * held
            terms.append(onto[:GROUP] + onto[GROUP:])
        for bit in (1, 2, 4):
            terms = [merge(low, high, bit) for low, high in zip(terms[::2], terms[1::2])]
        out[pl.ds(first, GROUP), :] = terms[0] + gain * value
        return held

    copy.wait()
    state[...] = lax.fori_loop(0, rows // GROUP, advance, begin[...].astype(jnp.float32))
    whole = out[...]
    ones = jnp.ones((squares.shape[0], width), jnp.float32)
    squares[...] = lax.dot_general(
        ones,
        whole * whole,
        (((1,), (1,)), ((), ())),
        precision=lax.Precision.HIGHEST,
        preferred_element_type=jnp.float32,
    )


def run_scan(source, half, rest, steps, maps, decay, skip, starts, copies):
    rows, width = half.shape
    cells = rows * width * decay.shape[0]
    return pl.pallas_call(
        scan_kernel,
        in_specs=[pl.BlockSpec(memory_space=pltpu.SMEM)]
        + [pl.BlockSpec(memory_space=pltpu.VMEM)] * 6
        + [pl.BlockSpec(memory_space=pl.ANY)],
        scratch_shapes=[
            pltpu.VMEM((rows, width), jnp.float32),
            pltpu.VMEM(starts.shape[1:], starts.dtype),
            pltpu.SemaphoreType.DMA,
        ],
        out_shape=(
            jax.ShapeDtypeStruct((rows, width), jnp.float32),
            jax.ShapeDtypeStruct(decay.shape, jnp.float32),
            jax.ShapeDtypeStruct((copies, rows), jnp.float32),
        ),
        compiler_params=pltpu.CompilerParams(vmem_limit_bytes=32 * 1024 * 1024),
        cost_estimate=pl.CostEstimate(flops=8 * cells, bytes_accessed=8 << 20, transcendentals=cells),
    )(source, half, rest, steps, maps, decay, skip, starts)


def join_kernel(weight, more_weight, token, more_token, weights, tokens):
    for out, parts in ((weights, (weight, more_weight)), (tokens, (token, more_token))):
        rows = parts[0].shape[0]
        for at in range(2):
            out[at * rows : (at + 1) * rows, :] = parts[at][...]


def run_join(*parts):
    shapes = [jax.ShapeDtypeStruct((2 * part.shape[0], part.shape[1]), part.dtype) for part in parts[::2]]
    return pl.pallas_call(
        join_kernel,
        out_shape=tuple(shapes),
        cost_estimate=pl.CostEstimate(flops=0, bytes_accessed=2 << 20, transcendentals=0),
    )(*parts)


def token_copies(blocks, backs, whole, landed):
    rows, part = blocks[0].shape[0] // 2, blocks[0].shape[1]
    copies = []
    for slot in range(8):
        for group in range(2):
            if slot < 5:
                source = blocks[slot].at[pl.ds(group * rows, rows), :]
            else:
                source = backs[7 - slot].at[pl.ds((1 - group) * rows, rows), :]
            at = 2 * slot + group
            copies.append(
                pltpu.make_async_copy(source, whole.at[:, pl.ds(at * part, part)], landed.at[at])
            )
    return copies


def narrow_kernel(where, down, maps, *rest):
    blocks, backs = rest[:5], rest[5:8]
    kept, sent, whole, picked, landed, taken = rest[8:]
    part = blocks[0].shape[1]
    rows = kept.shape[1]
    size = maps.shape[0]
    copies = token_copies(blocks, backs, whole, landed)
    takes = []
    for at in range(16):
        for side, ref in enumerate((down, maps)):
            takes.append(
                pltpu.make_async_copy(
                    ref.at[:, pl.ds(pl.multiple_of(where[at] * part, part), part)],
                    picked.at[pl.ds(side * size, size), pl.ds(at * part, part)],
                    taken.at[len(takes)],
                )
            )
    for copy in takes + copies:
        copy.start()
    for copy in takes + copies:
        copy.wait()
    for out, first in ((kept, 0), (sent, rows)):
        out[...] = lax.dot_general(
            picked[...],
            whole[first : first + rows, :],
            (((1,), (1,)), ((), ())),
            preferred_element_type=jnp.float32,
        )


def run_narrow(where, down, maps, blocks, backs):
    rows, part = blocks[0].shape[0] // 4, blocks[0].shape[1]
    free = pl.BlockSpec(memory_space=pl.ANY)
    one = jax.ShapeDtypeStruct((2 * maps.shape[0], rows), jnp.float32)
    return pl.pallas_call(
        narrow_kernel,
        in_specs=[pl.BlockSpec(memory_space=pltpu.SMEM)] + [free] * 10,
        out_shape=(one, one),
        scratch_shapes=[
            pltpu.VMEM((2 * rows, 16 * part), jnp.bfloat16),
            pltpu.VMEM((2 * maps.shape[0], 16 * part), jnp.bfloat16),
            pltpu.SemaphoreType.DMA((16,)),
            pltpu.SemaphoreType.DMA((32,)),
        ],
        compiler_params=pltpu.CompilerParams(vmem_limit_bytes=60 * 1024 * 1024),
        cost_estimate=pl.CostEstimate(flops=1 << 28, bytes_accessed=6 << 20, transcendentals=0),
    )(where, down, maps, *blocks, *backs)


def wide_kernel(where, column, *rest):
    blocks, backs = rest[:5], rest[5:8]
    kept, sent, whole, weights, total, landed, loaded = rest[8:]
    part = blocks[0].shape[1]
    rows = kept.shape[0]
    copies = token_copies(blocks, backs, whole, landed)
    loads = [
        pltpu.make_async_copy(
            column.at[pl.ds(pl.multiple_of(where[16 + at] * part, part), part), :],
            weights.at[pl.ds(at * part, part), :],
            loaded.at[at],
        )
        for at in range(16)
    ]
    for copy, load in zip(copies, loads):
        copy.start()
        load.start()
    for first in range(0, 16, 4):
        for at in range(first, first + 4):
            copies[at].wait()
            loads[at].wait()
        span = slice(first * part, (first + 4) * part)
        added = jnp.dot(whole[:, span], weights[span, :], preferred_element_type=jnp.float32)
        if first == 0:
            total[...] = added
        elif first < 12:
            total[...] += added
        else:
            added += total[...]
            kept[...] = added[:rows]
            sent[...] = added[rows:].astype(jnp.bfloat16)


def run_wide(where, column, blocks, backs):
    rows, part = blocks[0].shape[0] // 4, blocks[0].shape[1]
    width = column.shape[1]
    free = pl.BlockSpec(memory_space=pl.ANY)
    return pl.pallas_call(
        wide_kernel,
        in_specs=[pl.BlockSpec(memory_space=pltpu.SMEM)] + [free] * 9,
        out_shape=(
            jax.ShapeDtypeStruct((rows, width), jnp.float32),
            jax.ShapeDtypeStruct((rows, width), jnp.bfloat16),
        ),
        scratch_shapes=[
            pltpu.VMEM((2 * rows, 16 * part), jnp.bfloat16),
            pltpu.VMEM((16 * part, width), jnp.bfloat16),
            pltpu.VMEM((2 * rows, width), jnp.float32),
            pltpu.SemaphoreType.DMA((16,)),
            pltpu.SemaphoreType.DMA((16,)),
        ],
        compiler_params=pltpu.CompilerParams(vmem_limit_bytes=60 * 1024 * 1024),
        cost_estimate=pl.CostEstimate(flops=1 << 31, bytes_accessed=9 << 20, transcendentals=0),
    )(where, column, *blocks, *backs)


def per_device(
    tokens,
    w_inner,
    w_bc,
    w_dt_down,
    w_dt_up,
    step_bias,
    decay_rate,
    skip_gain,
    norm_gain,
    cache,
    hits,
):
    rows, share = tokens.shape
    depth, width = w_inner.shape
    parts = lax.axis_size("tp")
    chips = parts // 2
    lines = 4
    places = lax.axis_size("req")
    planes = places // lines
    state_size = decay_rate.shape[0]
    here, place = lax.axis_index("req"), lax.axis_index("tp")
    x, y, core = here & 3, place >> 1, place & 1
    along_z = [[lines * i + j for i in range(planes)] for j in range(lines)]
    across = [(i, i ^ 2) for i in range(places)]
    beside = [(i, i ^ 1) for i in range(places)]
    swap = [(i, i ^ 1) for i in range(parts)]
    onward = [(2 * i + c, (i + 1 - 2 * c) % chips * 2 + c) for i in range(chips) for c in range(2)]

    odd = x & 1
    mine = lax.dynamic_slice_in_dim(tokens, odd * depth, depth, axis=1)
    given = lax.dynamic_slice_in_dim(tokens, (1 - odd) * depth, depth, axis=1)
    column, own = run_join(
        w_inner, lax.ppermute(w_inner, "req", across), mine, lax.ppermute(given, "req", beside)
    )

    column = lax.all_gather(column, "req", axis=0, tiled=True, axis_index_groups=along_z)

    blocks = [jnp.concatenate([own, lax.ppermute(own, "tp", swap)], axis=0)]
    for turn in range(chips // 2):
        blocks.append(lax.ppermute(blocks[-1], "tp", onward))
    backs = [lax.ppermute(block, "tp", swap) for block in blocks[1:4]]

    at = jnp.arange(2 * chips, dtype=jnp.int32)
    chip = (y - (1 - 2 * core) * (at >> 1)) & 7
    side = core ^ (at & 1)
    where = jnp.concatenate([lines * chip + 2 * side + odd, 2 * chip + (side ^ (x >> 1))])

    states = jnp.take(cache[0].astype(jnp.bfloat16), hits[:, 1] - 1, axis=0, mode="clip")
    states = lax.all_to_all(states, "req", split_axis=0, concat_axis=0, tiled=True)
    source = lax.dynamic_slice_in_dim(hits[:, 0], here, 1)

    kept, sent = run_narrow(where, w_dt_down.T, w_bc.T, blocks, backs)
    narrow = kept + lax.ppermute(sent, "req", beside)
    half, sent = run_wide(where, column, blocks, backs)
    rest = lax.ppermute(sent, "req", beside)

    low = lax.all_gather(narrow[:32].astype(jnp.bfloat16), "tp", axis=0, tiled=True)
    spread = jnp.broadcast_to(jnp.transpose(narrow[32:])[:, :, None], (rows, 2 * state_size, 128))
    step = jax.nn.softplus(
        lax.dot_general(low, w_dt_up, (((0,), (0,)), ((), ())), preferred_element_type=jnp.float32)
        + step_bias[None, :]
    )
    out, state, squares = run_scan(
        source, half, rest, step, spread, decay_rate, skip_gain[None, :], states, parts
    )
    sums = jnp.sum(lax.all_to_all(squares, "tp", split_axis=0, concat_axis=0, tiled=True), axis=0)
    scale = lax.rsqrt(sums / (width * parts) + 1e-05)
    normed = (out * scale[:, None] * norm_gain[None, :]).astype(jnp.bfloat16)
    return (normed, state.reshape(1, state_size, width))


def solution(mesh):
    placed = (
        P("req", "tp"),
        P("req", "tp"),
        P(),
        P(None, "tp"),
        P(None, "tp"),
        P("tp"),
        P(None, "tp"),
        P("tp"),
        P("tp"),
        P("req", None, None, "tp"),
        P(),
    )
    return jax.shard_map(
        per_device,
        mesh=mesh,
        in_specs=placed,
        out_specs=(P("req", "tp"), P("req", None, "tp")),
        check_vma=False,
    )
```

```python
import jax
import jax.numpy as jnp
from jax import lax
from jax.experimental import pallas as pl
from jax.experimental.pallas import tpu as pltpu
from jax.sharding import PartitionSpec as P

LOG2E = 1.4426950408889634
GROUP = 8


def scan_kernel(source, half, rest, steps, maps, decay, skip, starts, out, state, squares, values, begin, landed):
    rows, width = out.shape
    copy = pltpu.make_async_copy(starts.at[source[0]], begin, landed)
    copy.start()
    projected = half[...] + rest[...].astype(jnp.float32)
    inner = projected / (1.0 + jnp.exp(-projected))
    values[...] = inner.astype(jnp.bfloat16).astype(jnp.float32)
    rate = decay[...] * -LOG2E
    size = decay.shape[0]
    gain = skip[...]
    line = lax.broadcasted_iota(jnp.int32, (GROUP, width), 0)

    def merge(low, high, bit):
        upper = (line & bit) != 0
        kept = jnp.where(upper, high, low)
        moved = jnp.where(upper, low, high)
        return kept + pltpu.roll(moved, GROUP - bit, 0)

    def advance(index, held):
        first = pl.multiple_of(index * GROUP, GROUP)
        value = values[pl.ds(first, GROUP), :]
        step = steps[pl.ds(first, GROUP), :]
        fed = step * value
        terms = []
        for at in range(GROUP):
            factor = jnp.exp2(rate * step[at : at + 1, :])
            into = jnp.tile(maps[first + at, :size], (1, width // 128))
            held = factor * held + into * fed[at : at + 1, :]
            onto = jnp.tile(maps[first + at, size:], (1, width // 128)) * held
            terms.append(onto[:GROUP] + onto[GROUP:])
        for bit in (1, 2, 4):
            terms = [merge(low, high, bit) for low, high in zip(terms[::2], terms[1::2])]
        out[pl.ds(first, GROUP), :] = terms[0] + gain * value
        return held

    copy.wait()
    state[...] = lax.fori_loop(0, rows // GROUP, advance, begin[...].astype(jnp.float32))
    square = out[...] * out[...]
    ones = jnp.ones((squares.shape[0], width), jnp.bfloat16)
    total = jnp.zeros(squares.shape, jnp.float32)
    for _ in range(3):
        high = square.astype(jnp.bfloat16)
        square -= high.astype(jnp.float32)
        total += lax.dot_general(
            ones, high, (((1,), (1,)), ((), ())), preferred_element_type=jnp.float32
        )
    squares[...] = total


def run_scan(source, half, rest, steps, maps, decay, skip, starts, copies):
    rows, width = half.shape
    cells = rows * width * decay.shape[0]
    return pl.pallas_call(
        scan_kernel,
        in_specs=[pl.BlockSpec(memory_space=pltpu.SMEM)]
        + [pl.BlockSpec(memory_space=pltpu.VMEM)] * 6
        + [pl.BlockSpec(memory_space=pl.ANY)],
        scratch_shapes=[
            pltpu.VMEM((rows, width), jnp.float32),
            pltpu.VMEM(starts.shape[1:], starts.dtype),
            pltpu.SemaphoreType.DMA,
        ],
        out_shape=(
            jax.ShapeDtypeStruct((rows, width), jnp.float32),
            jax.ShapeDtypeStruct(decay.shape, jnp.float32),
            jax.ShapeDtypeStruct((copies, rows), jnp.float32),
        ),
        compiler_params=pltpu.CompilerParams(vmem_limit_bytes=32 * 1024 * 1024),
        cost_estimate=pl.CostEstimate(flops=8 * cells, bytes_accessed=8 << 20, transcendentals=cells),
    )(source, half, rest, steps, maps, decay, skip, starts)


def join_kernel(weight, more_weight, token, more_token, weights, tokens):
    for out, parts in ((weights, (weight, more_weight)), (tokens, (token, more_token))):
        rows = parts[0].shape[0]
        for at in range(2):
            out[at * rows : (at + 1) * rows, :] = parts[at][...]


def run_join(*parts):
    shapes = [jax.ShapeDtypeStruct((2 * part.shape[0], part.shape[1]), part.dtype) for part in parts[::2]]
    return pl.pallas_call(
        join_kernel,
        out_shape=tuple(shapes),
        cost_estimate=pl.CostEstimate(flops=0, bytes_accessed=2 << 20, transcendentals=0),
    )(*parts)


def token_copies(blocks, backs, whole, landed):
    rows, part = blocks[0].shape[0] // 2, blocks[0].shape[1]
    copies = []
    for slot in range(8):
        for group in range(2):
            if slot < 5:
                source = blocks[slot].at[pl.ds(group * rows, rows), :]
            else:
                source = backs[7 - slot].at[pl.ds((1 - group) * rows, rows), :]
            at = 2 * slot + group
            copies.append(
                pltpu.make_async_copy(source, whole.at[:, pl.ds(at * part, part)], landed.at[at])
            )
    return copies


def project_kernel(where, down, maps, *rest):
    blocks, backs, column = rest[:5], rest[5:8], rest[8]
    narrow, narrow_sent, kept, sent, whole, thin, picked, weights, landed, taken, loaded = rest[9:]
    part = blocks[0].shape[1]
    rows = kept.shape[0]
    size = maps.shape[0]
    copies = token_copies(blocks, backs, whole, landed)
    takes = [pltpu.make_async_copy(ref, thin.at[at], taken.at[at]) for at, ref in enumerate((down, maps))]
    loads = [
        pltpu.make_async_copy(
            column.at[pl.ds(pl.multiple_of(where[16 + at] * part, part), part), :],
            weights.at[pl.ds(at * part, part), :],
            loaded.at[at],
        )
        for at in range(16)
    ]
    for copy in takes + copies + loads:
        copy.start()
    for take in takes:
        take.wait()
    for at in range(16):
        first = pl.multiple_of(where[at] * part, part)
        for side in range(2):
            picked[side * size : (side + 1) * size, at * part : (at + 1) * part] = thin[
                side, :, pl.ds(first, part)
            ]
    for copy in copies:
        copy.wait()
    for out, first in ((narrow, 0), (narrow_sent, rows)):
        out[...] = lax.dot_general(
            whole[first : first + rows, :],
            picked[...],
            (((1,), (1,)), ((), ())),
            preferred_element_type=jnp.float32,
        )
    for load in loads:
        load.wait()
    kept[...] = jnp.dot(whole[:rows, :], weights[...], preferred_element_type=jnp.float32)
    sent[...] = jnp.dot(whole[rows:, :], weights[...], preferred_element_type=jnp.float32).astype(
        jnp.bfloat16
    )


def run_project(where, down, maps, blocks, backs, column):
    rows, part = blocks[0].shape[0] // 4, blocks[0].shape[1]
    width = column.shape[1]
    free = pl.BlockSpec(memory_space=pl.ANY)
    one = jax.ShapeDtypeStruct((rows, 2 * maps.shape[0]), jnp.float32)
    return pl.pallas_call(
        project_kernel,
        in_specs=[pl.BlockSpec(memory_space=pltpu.SMEM)] + [free] * 11,
        out_shape=(
            one,
            one,
            jax.ShapeDtypeStruct((rows, width), jnp.float32),
            jax.ShapeDtypeStruct((rows, width), jnp.bfloat16),
        ),
        scratch_shapes=[
            pltpu.VMEM((2 * rows, 16 * part), jnp.bfloat16),
            pltpu.VMEM((2,) + maps.shape, jnp.bfloat16),
            pltpu.VMEM((2 * maps.shape[0], 16 * part), jnp.bfloat16),
            pltpu.VMEM((16 * part, width), jnp.bfloat16),
            pltpu.SemaphoreType.DMA((16,)),
            pltpu.SemaphoreType.DMA((2,)),
            pltpu.SemaphoreType.DMA((16,)),
        ],
        compiler_params=pltpu.CompilerParams(vmem_limit_bytes=60 * 1024 * 1024),
        cost_estimate=pl.CostEstimate(flops=1 << 31, bytes_accessed=9 << 20, transcendentals=0),
    )(where, down, maps, *blocks, *backs, column)


def per_device(
    tokens,
    w_inner,
    w_bc,
    w_dt_down,
    w_dt_up,
    step_bias,
    decay_rate,
    skip_gain,
    norm_gain,
    cache,
    hits,
):
    rows, share = tokens.shape
    depth, width = w_inner.shape
    parts = lax.axis_size("tp")
    chips = parts // 2
    lines = 4
    places = lax.axis_size("req")
    planes = places // lines
    state_size = decay_rate.shape[0]
    here, place = lax.axis_index("req"), lax.axis_index("tp")
    x, y, core = here & 3, place >> 1, place & 1
    along_z = [[lines * i + j for i in range(planes)] for j in range(lines)]
    across = [(i, i ^ 2) for i in range(places)]
    beside = [(i, i ^ 1) for i in range(places)]
    swap = [(i, i ^ 1) for i in range(parts)]
    onward = [(2 * i + c, (i + 1 - 2 * c) % chips * 2 + c) for i in range(chips) for c in range(2)]

    odd = x & 1
    mine = lax.dynamic_slice_in_dim(tokens, odd * depth, depth, axis=1)
    given = lax.dynamic_slice_in_dim(tokens, (1 - odd) * depth, depth, axis=1)
    column, own = run_join(
        w_inner, lax.ppermute(w_inner, "req", across), mine, lax.ppermute(given, "req", beside)
    )

    column = lax.all_gather(column, "req", axis=0, tiled=True, axis_index_groups=along_z)

    blocks = [jnp.concatenate([own, lax.ppermute(own, "tp", swap)], axis=0)]
    for turn in range(chips // 2):
        blocks.append(lax.ppermute(blocks[-1], "tp", onward))
    backs = [lax.ppermute(block, "tp", swap) for block in blocks[1:4]]

    at = jnp.arange(2 * chips, dtype=jnp.int32)
    chip = (y - (1 - 2 * core) * (at >> 1)) & 7
    side = core ^ (at & 1)
    where = jnp.concatenate([lines * chip + 2 * side + odd, 2 * chip + (side ^ (x >> 1))])

    states = jnp.take(cache[0].astype(jnp.bfloat16), hits[:, 1] - 1, axis=0, mode="clip")
    states = lax.all_to_all(states, "req", split_axis=0, concat_axis=0, tiled=True)
    source = lax.dynamic_slice_in_dim(hits[:, 0], here, 1)

    narrow, narrow_sent, half, sent = run_project(
        where, w_dt_down.T, w_bc.T, blocks, backs, column
    )
    narrow = narrow + lax.ppermute(narrow_sent, "req", beside)
    rest = lax.ppermute(sent, "req", beside)
    low = lax.all_gather(narrow[:, :32].astype(jnp.bfloat16), "tp", axis=1, tiled=True)
    spread = jnp.broadcast_to(narrow[:, 32:, None], (rows, 2 * state_size, 128))
    step = jax.nn.softplus(
        jnp.dot(low, w_dt_up, preferred_element_type=jnp.float32) + step_bias[None, :]
    )
    out, state, squares = run_scan(
        source, half, rest, step, spread, decay_rate, skip_gain[None, :], states, parts
    )
    sums = jnp.sum(lax.all_to_all(squares, "tp", split_axis=0, concat_axis=0, tiled=True), axis=0)
    scale = lax.rsqrt(sums / (width * parts) + 1e-05)
    normed = (out * scale[:, None] * norm_gain[None, :]).astype(jnp.bfloat16)
    return (normed, state.reshape(1, state_size, width))


def solution(mesh):
    placed = (
        P("req", "tp"),
        P("req", "tp"),
        P(),
        P(None, "tp"),
        P(None, "tp"),
        P("tp"),
        P(None, "tp"),
        P("tp"),
        P("tp"),
        P("req", None, None, "tp"),
        P(),
    )
    return jax.shard_map(
        per_device,
        mesh=mesh,
        in_specs=placed,
        out_specs=(P("req", "tp"), P("req", None, "tp")),
        check_vma=False,
    )
```

```python
import jax
import jax.numpy as jnp
from jax import lax
from jax.experimental import pallas as pl
from jax.experimental.pallas import tpu as pltpu
from jax.sharding import PartitionSpec as P

LOG2E = 1.4426950408889634
GROUP = 8


def scan_kernel(source, half, rest, steps, maps, decay, skip, starts, out, state, squares, values, begin, landed):
    rows, width = out.shape
    copy = pltpu.make_async_copy(starts.at[source[0]], begin, landed)
    copy.start()
    projected = half[...] + rest[...].astype(jnp.float32)
    inner = projected / (1.0 + jnp.exp(-projected))
    values[...] = inner.astype(jnp.bfloat16).astype(jnp.float32)
    rate = decay[...] * -LOG2E
    size = decay.shape[0]
    gain = skip[...]
    line = lax.broadcasted_iota(jnp.int32, (GROUP, width), 0)

    def merge(low, high, bit):
        upper = (line & bit) != 0
        kept = jnp.where(upper, high, low)
        moved = jnp.where(upper, low, high)
        return kept + pltpu.roll(moved, GROUP - bit, 0)

    def advance(index, held):
        first = pl.multiple_of(index * GROUP, GROUP)
        value = values[pl.ds(first, GROUP), :]
        step = steps[pl.ds(first, GROUP), :]
        fed = step * value
        terms = []
        for at in range(GROUP):
            factor = jnp.exp2(rate * step[at : at + 1, :])
            into = jnp.tile(maps[first + at, :size], (1, width // 128))
            held = factor * held + into * fed[at : at + 1, :]
            onto = jnp.tile(maps[first + at, size:], (1, width // 128)) * held
            terms.append(onto[:GROUP] + onto[GROUP:])
        for bit in (1, 2, 4):
            terms = [merge(low, high, bit) for low, high in zip(terms[::2], terms[1::2])]
        out[pl.ds(first, GROUP), :] = terms[0] + gain * value
        return held

    copy.wait()
    state[...] = lax.fori_loop(0, rows // GROUP, advance, begin[...].astype(jnp.float32))
    square = out[...] * out[...]
    ones = jnp.ones((squares.shape[0], width), jnp.bfloat16)
    total = jnp.zeros(squares.shape, jnp.float32)
    for _ in range(3):
        high = square.astype(jnp.bfloat16)
        square -= high.astype(jnp.float32)
        total += lax.dot_general(
            ones, high, (((1,), (1,)), ((), ())), preferred_element_type=jnp.float32
        )
    squares[...] = total


def run_scan(source, half, rest, steps, maps, decay, skip, starts, copies):
    rows, width = half.shape
    cells = rows * width * decay.shape[0]
    return pl.pallas_call(
        scan_kernel,
        in_specs=[pl.BlockSpec(memory_space=pltpu.SMEM)]
        + [pl.BlockSpec(memory_space=pltpu.VMEM)] * 6
        + [pl.BlockSpec(memory_space=pl.ANY)],
        scratch_shapes=[
            pltpu.VMEM((rows, width), jnp.float32),
            pltpu.VMEM(starts.shape[1:], starts.dtype),
            pltpu.SemaphoreType.DMA,
        ],
        out_shape=(
            jax.ShapeDtypeStruct((rows, width), jnp.float32),
            jax.ShapeDtypeStruct(decay.shape, jnp.float32),
            jax.ShapeDtypeStruct((copies, rows), jnp.float32),
        ),
        compiler_params=pltpu.CompilerParams(vmem_limit_bytes=32 * 1024 * 1024),
        cost_estimate=pl.CostEstimate(flops=8 * cells, bytes_accessed=8 << 20, transcendentals=cells),
    )(source, half, rest, steps, maps, decay, skip, starts)


def join_kernel(weight, more_weight, token, more_token, weights, tokens):
    for out, parts in ((weights, (weight, more_weight)), (tokens, (token, more_token))):
        rows = parts[0].shape[0]
        for at in range(2):
            out[at * rows : (at + 1) * rows, :] = parts[at][...]


def run_join(*parts):
    shapes = [jax.ShapeDtypeStruct((2 * part.shape[0], part.shape[1]), part.dtype) for part in parts[::2]]
    return pl.pallas_call(
        join_kernel,
        out_shape=tuple(shapes),
        cost_estimate=pl.CostEstimate(flops=0, bytes_accessed=2 << 20, transcendentals=0),
    )(*parts)


def token_copies(blocks, backs, whole, landed):
    rows, part = blocks[0].shape[0] // 2, blocks[0].shape[1]
    copies = []
    for slot in range(8):
        for group in range(2):
            if slot < 5:
                source = blocks[slot].at[pl.ds(group * rows, rows), :]
            else:
                source = backs[7 - slot].at[pl.ds((1 - group) * rows, rows), :]
            at = 2 * slot + group
            copies.append(
                pltpu.make_async_copy(source, whole.at[:, pl.ds(at * part, part)], landed.at[at])
            )
    return copies


def project_kernel(where, down, maps, *rest):
    blocks, backs, column = rest[:5], rest[5:8], rest[8]
    narrow, narrow_sent, kept, sent, whole, thin, picked, weights, total, landed, taken, loaded = rest[9:]
    part = blocks[0].shape[1]
    rows = kept.shape[0]
    size = maps.shape[0]
    copies = token_copies(blocks, backs, whole, landed)
    takes = [pltpu.make_async_copy(ref, thin.at[at], taken.at[at]) for at, ref in enumerate((down, maps))]
    loads = [
        pltpu.make_async_copy(
            column.at[pl.ds(pl.multiple_of(where[16 + at] * part, part), part), :],
            weights.at[pl.ds(at * part, part), :],
            loaded.at[at],
        )
        for at in range(16)
    ]
    for first in range(0, 16, 8):
        for copy in copies[first : first + 8] + loads[first : first + 8]:
            copy.start()
    for take in takes:
        take.start()
    for copy in copies[:8] + loads[:8]:
        copy.wait()
    span = 8 * part
    kept[...] = jnp.dot(whole[:rows, :span], weights[:span, :], preferred_element_type=jnp.float32)
    total[...] = jnp.dot(whole[rows:, :span], weights[:span, :], preferred_element_type=jnp.float32)
    for copy in copies[8:] + loads[8:]:
        copy.wait()
    kept[...] += jnp.dot(whole[:rows, span:], weights[span:, :], preferred_element_type=jnp.float32)
    more = jnp.dot(whole[rows:, span:], weights[span:, :], preferred_element_type=jnp.float32)
    sent[...] = (total[...] + more).astype(jnp.bfloat16)
    for take in takes:
        take.wait()
    for at in range(16):
        first = pl.multiple_of(where[at] * part, part)
        for side in range(2):
            picked[side * size : (side + 1) * size, at * part : (at + 1) * part] = thin[
                side, :, pl.ds(first, part)
            ]
    for out, first in ((narrow, 0), (narrow_sent, rows)):
        out[...] = lax.dot_general(
            whole[first : first + rows, :],
            picked[...],
            (((1,), (1,)), ((), ())),
            preferred_element_type=jnp.float32,
        )


def run_project(where, down, maps, blocks, backs, column):
    rows, part = blocks[0].shape[0] // 4, blocks[0].shape[1]
    width = column.shape[1]
    free = pl.BlockSpec(memory_space=pl.ANY)
    one = jax.ShapeDtypeStruct((rows, 2 * maps.shape[0]), jnp.float32)
    return pl.pallas_call(
        project_kernel,
        in_specs=[pl.BlockSpec(memory_space=pltpu.SMEM)] + [free] * 11,
        out_shape=(
            one,
            one,
            jax.ShapeDtypeStruct((rows, width), jnp.float32),
            jax.ShapeDtypeStruct((rows, width), jnp.bfloat16),
        ),
        scratch_shapes=[
            pltpu.VMEM((2 * rows, 16 * part), jnp.bfloat16),
            pltpu.VMEM((2,) + maps.shape, jnp.bfloat16),
            pltpu.VMEM((2 * maps.shape[0], 16 * part), jnp.bfloat16),
            pltpu.VMEM((16 * part, width), jnp.bfloat16),
            pltpu.VMEM((rows, width), jnp.float32),
            pltpu.SemaphoreType.DMA((16,)),
            pltpu.SemaphoreType.DMA((2,)),
            pltpu.SemaphoreType.DMA((16,)),
        ],
        compiler_params=pltpu.CompilerParams(vmem_limit_bytes=60 * 1024 * 1024),
        cost_estimate=pl.CostEstimate(flops=1 << 31, bytes_accessed=9 << 20, transcendentals=0),
    )(where, down, maps, *blocks, *backs, column)


def per_device(
    tokens,
    w_inner,
    w_bc,
    w_dt_down,
    w_dt_up,
    step_bias,
    decay_rate,
    skip_gain,
    norm_gain,
    cache,
    hits,
):
    rows, share = tokens.shape
    depth, width = w_inner.shape
    parts = lax.axis_size("tp")
    chips = parts // 2
    lines = 4
    places = lax.axis_size("req")
    planes = places // lines
    state_size = decay_rate.shape[0]
    here, place = lax.axis_index("req"), lax.axis_index("tp")
    x, y, core = here & 3, place >> 1, place & 1
    along_z = [[lines * i + j for i in range(planes)] for j in range(lines)]
    across = [(i, i ^ 2) for i in range(places)]
    beside = [(i, i ^ 1) for i in range(places)]
    swap = [(i, i ^ 1) for i in range(parts)]
    onward = [(2 * i + c, (i + 1 - 2 * c) % chips * 2 + c) for i in range(chips) for c in range(2)]

    odd = x & 1
    mine = lax.dynamic_slice_in_dim(tokens, odd * depth, depth, axis=1)
    given = lax.dynamic_slice_in_dim(tokens, (1 - odd) * depth, depth, axis=1)
    column, own = run_join(
        w_inner, lax.ppermute(w_inner, "req", across), mine, lax.ppermute(given, "req", beside)
    )

    column = lax.all_gather(column, "req", axis=0, tiled=True, axis_index_groups=along_z)

    blocks = [jnp.concatenate([own, lax.ppermute(own, "tp", swap)], axis=0)]
    for turn in range(chips // 2):
        blocks.append(lax.ppermute(blocks[-1], "tp", onward))
    backs = [lax.ppermute(block, "tp", swap) for block in blocks[1:4]]

    at = jnp.arange(2 * chips, dtype=jnp.int32)
    chip = (y - (1 - 2 * core) * (at >> 1)) & 7
    side = core ^ (at & 1)
    where = jnp.concatenate([lines * chip + 2 * side + odd, 2 * chip + (side ^ (x >> 1))])

    states = jnp.take(cache[0].astype(jnp.bfloat16), hits[:, 1] - 1, axis=0, mode="clip")
    states = lax.all_to_all(states, "req", split_axis=0, concat_axis=0, tiled=True)
    source = lax.dynamic_slice_in_dim(hits[:, 0], here, 1)

    narrow, narrow_sent, half, sent = run_project(
        where, w_dt_down.T, w_bc.T, blocks, backs, column
    )
    narrow = narrow + lax.ppermute(narrow_sent, "req", beside)
    rest = lax.ppermute(sent, "req", beside)
    low = lax.all_gather(narrow[:, :32].astype(jnp.bfloat16), "tp", axis=1, tiled=True)
    spread = jnp.broadcast_to(narrow[:, 32:, None], (rows, 2 * state_size, 128))
    step = jax.nn.softplus(
        jnp.dot(low, w_dt_up, preferred_element_type=jnp.float32) + step_bias[None, :]
    )
    out, state, squares = run_scan(
        source, half, rest, step, spread, decay_rate, skip_gain[None, :], states, parts
    )
    sums = jnp.sum(lax.all_to_all(squares, "tp", split_axis=0, concat_axis=0, tiled=True), axis=0)
    scale = lax.rsqrt(sums / (width * parts) + 1e-05)
    normed = (out * scale[:, None] * norm_gain[None, :]).astype(jnp.bfloat16)
    return (normed, state.reshape(1, state_size, width))


def solution(mesh):
    placed = (
        P("req", "tp"),
        P("req", "tp"),
        P(),
        P(None, "tp"),
        P(None, "tp"),
        P("tp"),
        P(None, "tp"),
        P("tp"),
        P("tp"),
        P("req", None, None, "tp"),
        P(),
    )
    return jax.shard_map(
        per_device,
        mesh=mesh,
        in_specs=placed,
        out_specs=(P("req", "tp"), P("req", None, "tp")),
        check_vma=False,
    )
```
